32 devices in a mesh: groups: 2 (over y), lon: 4 (over x, core), lat: 4 (over z).
Axes of the slice: x: 2, y: 2, z: 4, core: 2. Of those that a mesh axis runs over, the one named last changes fastest.
Arguments:
- node_latent: bfloat16 [16384, 512], P(('groups', 'lon', 'lat')), parts along dimension 0, may hold values from -6 to 6
- fine_edges: bfloat16 [98304, 512], P(('groups', 'lon', 'lat')), parts along dimension 0, may hold values from -6 to 6
- coarse_edges: bfloat16 [32768, 512], P(('groups', 'lon', 'lat')), parts along dimension 0, may hold values from -6 to 6
- fine_sender: int32 [98304], P(('groups', 'lon', 'lat')), parts along dimension 0, may hold values from 0 to 8191, as said below
- fine_receiver: int32 [98304], P(('groups', 'lon', 'lat')), parts along dimension 0, may hold values from 0 to 511
- coarse_peer: int32 [32768, 1], P(('groups', 'lon', 'lat')), parts along dimension 0, may hold values from 0 to 15; in each aligned block of 1024 rows (0 to 1023, 1024 to 2047, ...) at most 128 rows name the same one
- coarse_row: int32 [32768], P(('groups', 'lon', 'lat')), parts along dimension 0, may hold values from 0 to 127
- coarse_receiver: int32 [32768], P(('groups', 'lon', 'lat')), parts along dimension 0, may hold values from 0 to 511
- edge_in: bfloat16 [1536, 512], replicated, may hold values from -0.15625 to 0.15625
- edge_out: bfloat16 [512, 512], replicated, may hold values from -0.25 to 0.25
- edge_gain: float32 [512], replicated, may hold values from 0.1 to 1.9
- node_in: bfloat16 [1024, 512], replicated, may hold values from -0.1875 to 0.1875
- node_out: bfloat16 [512, 512], replicated, may hold values from -0.25 to 0.25
- node_gain: float32 [512], replicated, may hold values from 0.1 to 1.9
Outputs:
- node_next: bfloat16 [16384, 512], P(('groups', 'lon', 'lat')), parts along dimension 0
- fine_next: bfloat16 [98304, 512], P(('groups', 'lon', 'lat')), parts along dimension 0
- coarse_next: bfloat16 [32768, 512], P(('groups', 'lon', 'lat')), parts along dimension 0
The draws below stay inside these ranges and needn't reach their ends.
There are 2 independent parts, one for each index of `groups`. The reference program is written for one: setup_inputs(seed, part) draws one part's arguments, and reference() takes and returns one part's arrays. A program takes and returns all parts, laid end to end along the dimension named above; an argument that names none is the same for every part. Nothing has to cross between parts.
Inputs may be any that keep to these rules, and one draw needn't show every extreme that they name: `fine_sender`: A partition's row r lies at grid place (r // 16, r % 16) of a 32 x 16 local grid, the first coordinate along longitude. The sender of a finest-level edge lies in the edge's own partition or in one of the eight partitions beside it: longitude sector one lower, equal or one higher (sectors wrap around), latitude band one lower, equal or one higher (bands do not wrap); partition index = sector index * number of bands + band index. A sender in the sector one lower has first coordinate 32 - 1, in the sector one higher first coordinate 0; a sender in the band one lower has second coordinate 16 - 1, in the band one higher second coordinate 0. `coarse_peer`: among the 1024 coarser-level edges of one partition, at most 128 name the same sender partition.
All inputs are finite; a program needn't handle non-finite values.
Results may differ from the reference program's by a relative error of at most 0.0053.
Values may be sent and summed in bfloat16 or wider, within the bound.
A program may use at most 128 MiB of HBM per device.

```python
import math
import jax
import jax.numpy as jnp
import numpy as np
from jax import lax

D = 512
HID = 512
NODE_DEV = 512
GRID_LAT = 16
PARTS_SIZE = 16
COARSE_DEV = 128
FINE_DEV = 3072
COARSE_EDGE_DEV = 1024
CAP = 128
NODES = 8192
FINE_EDGES = 49152
COARSE_EDGES = 16384
N_LON = 4
N_LAT = 4


def draw_fine_sender(key, part):
    key = jax.random.fold_in(key, 11)
    keys = jax.random.split(key, 6)
    owner = jnp.arange(FINE_EDGES, dtype=jnp.int32) // FINE_DEV
    sector = owner // N_LAT
    band = owner % N_LAT
    crossing = jax.random.randint(keys[0], (FINE_EDGES,), 0, 100, dtype=jnp.int32) < 18
    face = jax.random.randint(keys[1], (FINE_EDGES,), 0, 4, dtype=jnp.int32)
    corner_pick = jax.random.randint(keys[2], (FINE_EDGES,), 0, 4, dtype=jnp.int32)
    is_corner = jax.random.randint(keys[3], (FINE_EDGES,), 0, 6, dtype=jnp.int32) == 0
    face_lon = jnp.where(face == 0, -1, jnp.where(face == 1, 1, 0))
    face_lat = jnp.where(face == 2, -1, jnp.where(face == 3, 1, 0))
    corner_lon = jnp.where(corner_pick < 2, -1, 1)
    corner_lat = jnp.where(corner_pick % 2 == 0, -1, 1)
    lon_step = jnp.where(is_corner, corner_lon, face_lon)
    lat_step = jnp.where(is_corner, corner_lat, face_lat)
    lon_step = jnp.where(crossing, lon_step, 0)
    lat_step = jnp.where(crossing, lat_step, 0)
    moved = band + lat_step
    outside = (moved < 0) | (moved >= N_LAT)
    lat_step = jnp.where(outside, -lat_step, lat_step)
    moved = band + lat_step
    grid_lon = NODE_DEV // GRID_LAT
    free_i = jax.random.randint(keys[4], (FINE_EDGES,), 0, grid_lon, dtype=jnp.int32)
    free_j = jax.random.randint(keys[5], (FINE_EDGES,), 0, GRID_LAT, dtype=jnp.int32)
    place_i = jnp.where(lon_step == -1, grid_lon - 1, jnp.where(lon_step == 1, 0, free_i))
    place_j = jnp.where(lat_step == -1, GRID_LAT - 1, jnp.where(lat_step == 1, 0, free_j))
    row_pick = place_i * GRID_LAT + place_j
    source = (sector + lon_step + N_LON) % N_LON * N_LAT + moved
    return (source * NODE_DEV + row_pick).astype(jnp.int32)


def with_ends(entries, own_key, least, high):
    longest = entries.shape.index(max(entries.shape))
    spots = []
    for shift in (0, 1):
        where = [jax.random.randint(jax.random.fold_in(own_key, axis), (), 0, length) for axis, length in enumerate(entries.shape)]
        where[longest] = (where[longest] + shift) % entries.shape[longest]
        spots.append(tuple(where))
    return entries.at[spots[0]].set(least).at[spots[1]].set(high)


def block_levels(rng, extent, shards, smallest, largest):
    level, own = 1.0, jax.random.fold_in(rng, 6)
    for dim, blocks in shards:
        heights = jnp.exp(jax.random.uniform(jax.random.fold_in(own, dim), (blocks,), jnp.float32, smallest / len(shards), largest / len(shards)))
        level = level * jnp.repeat(heights, extent[dim] // blocks).reshape([-1 if axis == dim else 1 for axis in range(len(extent))])
    return level


def assign_block(key, own, number, rows, count, top, limit, lean):
    order = jax.random.permutation(key, count)
    heavy_load, ordinary = shares(count, rows * top, limit, lean, True), shares(count, rows * top, limit, lean, False)
    places = jnp.arange(count)

    def named(sizes, turn):
        used = int((sizes > 0).sum())
        fixed = max(1, used // 4)
        shifted = fixed + (places - fixed + turn * (used - fixed)) % max(1, count - fixed)
        return jnp.zeros((count,), jnp.int32).at[order[jnp.where(places < fixed, places, shifted)]].set(jnp.asarray(sizes, jnp.int32))

    sizes = jnp.where(number % 4 == 0, named(heavy_load, number // 4), named(ordinary, number - number // 4 - 1))
    mixed = jax.random.permutation(jax.random.fold_in(own, 3), count)
    source_of, receiver = mixed[0:count // 2 * 2:2], mixed[1:count // 2 * 2:2]
    slack = jnp.minimum(sizes[source_of] - 1, limit - sizes[receiver]) // 2
    slack = jnp.where((source_of == order[0]) | (receiver == order[0]) | (sizes[receiver] == 0), 0, jnp.maximum(slack, 0))
    shifted = jax.random.randint(jax.random.fold_in(own, 4), (count // 2,), 0, 1 << 20) % (slack + 1)
    sizes = sizes.at[source_of].add(-shifted).at[receiver].add(shifted)
    items = jnp.searchsorted(jnp.cumsum(sizes), jnp.arange(rows * top), side="right").astype(jnp.int32)
    table = items.reshape(top, rows).T
    table = table[jax.random.permutation(jax.random.fold_in(own, 1), rows)]
    turn = jax.random.randint(jax.random.fold_in(own, 2), (rows, 1), 0, top)
    return jnp.take_along_axis(table, (jnp.arange(top)[None, :] + turn) % top, axis=1)


def shares(amount, total, limit, lean, full):
    weights = [(1 << 20) // math.isqrt(standing ** lean) + 1 for standing in range(1, amount + 1)]
    largest = limit if full else min(limit, max(-(-total // amount), total * weights[0] // sum(weights)))
    least = 1 if total - largest >= amount - 1 else 0
    holding, rest = [largest] + [least] * (amount - 1), total - largest - least * (amount - 1)
    while rest > 0:
        candidates = [i for i in range(1, amount) if holding[i] < largest] or [i for i in range(1, amount) if holding[i] < limit]
        whole, budget = sum([weights[i] for i in candidates]), rest
        for i in candidates:
            more = min(limit - holding[i], max(1, budget * weights[i] // whole), rest)
            holding[i] = holding[i] + more
            rest = rest - more
    return np.array(holding)


def gaussian(rng, shape, scale, limit, cuts=(), held_as=jnp.bfloat16):
    array = jax.random.normal(rng, shape, jnp.float32) * scale
    if len(cuts) > 0:
        array = block_levels(rng, shape, cuts, -0.22, 0.18) * array
    return jnp.clip(array, min=-limit, max=limit).astype(held_as)


def setup_inputs(seed: int = 0, part: int = 0) -> dict:
    arg_keys = jax.random.split(jax.random.key(seed), 15)
    own_keys = jax.random.split(jax.random.fold_in(arg_keys[14], part), 15)
    node_latent = gaussian(own_keys[0], (NODES, D), 1.0, 6.0, ((0, 16),))
    fine_edges = gaussian(own_keys[1], (FINE_EDGES, D), 1.0, 6.0, ((0, 16),))
    coarse_edges = gaussian(own_keys[2], (COARSE_EDGES, D), 1.0, 6.0, ((0, 16),))
    fine_sender = draw_fine_sender(jax.random.fold_in(jax.random.fold_in(arg_keys[14], part), 71), part)
    fine_receiver = with_ends(jax.random.randint(own_keys[4], (FINE_EDGES,), 0, NODE_DEV), jax.random.fold_in(own_keys[4], 1), 0, NODE_DEV - 1).astype(jnp.int32)
    coarse_peer_keys = jax.random.split(jax.random.fold_in(own_keys[5], 1), COARSE_EDGES // COARSE_EDGE_DEV)
    coarse_peer_turns = jax.random.permutation(jax.random.fold_in(own_keys[5], 3), COARSE_EDGES // COARSE_EDGE_DEV)
    coarse_peer = jax.vmap(lambda own, number: assign_block(jax.random.fold_in(own_keys[5], 2), own, number, COARSE_EDGE_DEV, PARTS_SIZE, 1, CAP, 1))(coarse_peer_keys, coarse_peer_turns).reshape((COARSE_EDGES, 1))
    coarse_row = with_ends(jax.random.randint(own_keys[6], (COARSE_EDGES,), 0, COARSE_DEV), jax.random.fold_in(own_keys[6], 1), 0, COARSE_DEV - 1).astype(jnp.int32)
    coarse_receiver = with_ends(jax.random.randint(own_keys[7], (COARSE_EDGES,), 0, NODE_DEV), jax.random.fold_in(own_keys[7], 1), 0, NODE_DEV - 1).astype(jnp.int32)
    edge_in = gaussian(arg_keys[8], (3 * D, HID), (3 * D) ** -0.5, 0.15625)
    edge_out = gaussian(arg_keys[9], (HID, D), HID ** -0.5, 0.25)
    edge_gain = jnp.clip(1.0 + 0.18 * jax.random.normal(arg_keys[10], (D,), jnp.float32), 0.1, 1.9)
    node_in = gaussian(arg_keys[11], (2 * D, HID), (2 * D) ** -0.5, 0.1875)
    node_out = gaussian(arg_keys[12], (HID, D), HID ** -0.5, 0.25)
    node_gain = jnp.clip(1.0 + 0.18 * jax.random.normal(arg_keys[13], (D,), jnp.float32), 0.1, 1.9)
    return dict(node_latent=node_latent, fine_edges=fine_edges, coarse_edges=coarse_edges, fine_sender=fine_sender, fine_receiver=fine_receiver, coarse_peer=coarse_peer, coarse_row=coarse_row, coarse_receiver=coarse_receiver, edge_in=edge_in, edge_out=edge_out, edge_gain=edge_gain, node_in=node_in, node_out=node_out, node_gain=node_gain)


def layer_norm(values, gain):
    mean = lax.optimization_barrier(jnp.mean(values, axis=-1, keepdims=True))
    centred = values - mean
    scale = lax.rsqrt(lax.optimization_barrier(jnp.mean(centred * centred, axis=-1, keepdims=True)) + 1e-05)
    return centred * scale * gain

def edge_update(edges, senders, receivers, edge_in, edge_out, edge_gain):
    joined = jnp.concatenate([edges, senders, receivers], axis=1)
    hidden = jax.nn.silu(jnp.dot(joined, edge_in, preferred_element_type=jnp.float32)).astype(jnp.bfloat16)
    update = layer_norm(jnp.dot(hidden, edge_out, preferred_element_type=jnp.float32), edge_gain)
    message = update.astype(jnp.bfloat16)
    new_edges = (edges.astype(jnp.float32) + update).astype(jnp.bfloat16)
    return (message, new_edges)

def reference(node_latent, fine_edges, coarse_edges, fine_sender, fine_receiver, coarse_peer, coarse_row, coarse_receiver, edge_in, edge_out, edge_gain, node_in, node_out, node_gain):
    parts = N_LON * N_LAT
    fine_owner = jnp.arange(FINE_EDGES, dtype=jnp.int32) // FINE_DEV
    fine_target = fine_owner * NODE_DEV + fine_receiver
    coarse_owner = jnp.arange(COARSE_EDGES, dtype=jnp.int32) // COARSE_EDGE_DEV
    coarse_target = coarse_owner * NODE_DEV + coarse_receiver
    coarse_source = coarse_peer[:, 0] * NODE_DEV + coarse_row

    def run_edges(edges, senders, receivers):

        def one_block(pieces):
            block_edges, block_send, block_recv = pieces
            return edge_update(block_edges, node_latent[block_send], node_latent[block_recv], edge_in, edge_out, edge_gain)
        message, new_edges = lax.map(one_block, (edges.reshape(parts, -1, D), senders.reshape(parts, -1), receivers.reshape(parts, -1)))
        return (message.reshape(-1, D), new_edges.reshape(-1, D))
    fine_message, fine_next = run_edges(fine_edges, fine_sender, fine_target)
    coarse_message, coarse_next = run_edges(coarse_edges, coarse_source, coarse_target)
    gathered = jax.ops.segment_sum(fine_message.astype(jnp.float32), fine_target, num_segments=NODES)
    gathered = gathered + jax.ops.segment_sum(coarse_message.astype(jnp.float32), coarse_target, num_segments=NODES)
    gathered = gathered.astype(jnp.bfloat16)
    joined = jnp.concatenate([node_latent, gathered], axis=1)
    hidden = jax.nn.silu(jnp.dot(joined, node_in, preferred_element_type=jnp.float32)).astype(jnp.bfloat16)
    update = layer_norm(jnp.dot(hidden, node_out, preferred_element_type=jnp.float32), node_gain)
    node_next = (node_latent.astype(jnp.float32) + update).astype(jnp.bfloat16)
    return (node_next, fine_next, coarse_next)
```

```python
import jax
import jax.numpy as jnp
from jax import lax
from jax.experimental import pallas as pl
from jax.experimental.pallas import tpu as pltpu
from jax.sharding import PartitionSpec as P

GRID_LAT = 16
MESH = pl.DeviceIdType.MESH
GROUP = 128
TILE = 512
SUB = 256
RIM_LON = 16
RIM_LAT = 32
HALO = 256


def one_hot(rows, width):
    lanes = lax.broadcasted_iota(jnp.int32, (GROUP, GROUP), 1).astype(jnp.float32)
    tall = []
    for row in rows:
        column = jnp.transpose(jnp.broadcast_to(row, (GROUP, GROUP)))
        tall.append(
            jnp.concatenate(
                [
                    jnp.where(column == lanes + float(first), 1.0, 0.0).astype(jnp.bfloat16)
                    for first in range(0, width, GROUP)
                ],
                axis=1,
            )
        )
    return jnp.concatenate(tall, axis=0)


def one_hot_across(rows, height):
    places = lax.broadcasted_iota(jnp.int32, (height, GROUP), 0).astype(jnp.float32)
    return jnp.concatenate(
        [jnp.where(places == row, 1.0, 0.0).astype(jnp.bfloat16) for row in rows], axis=1
    )


def matmul(a, b):
    return jnp.dot(a, b, preferred_element_type=jnp.float32)


def silu_of_twice(half):
    return (half * (1.0 + jnp.tanh(half))).astype(jnp.bfloat16)


def normed(values, gain):
    scale = 1.0 / values.shape[-1]
    mean = jnp.sum(values, axis=-1, keepdims=True) * scale
    centred = values - mean
    square = jnp.sum(centred * centred, axis=-1, keepdims=True) * scale
    return centred * lax.rsqrt(square + 1e-05) * gain


def fine_kernel(
    node_ref,
    edges_ref,
    sender_ref,
    receiver_ref,
    edge_in_ref,
    edge_out_ref,
    gain_ref,
    message_ref,
    total_ref,
    every_ref,
    recv_table_ref,
    table,
    rims,
    edge_half,
    edge_buf,
    message_buf,
    sender_ids,
    receiver_ids,
    edge_sem,
    message_sem,
    own_sem,
    halo_send,
    halo_recv,
    send_sem,
    recv_sem,
):
    nodes, width = node_ref.shape
    tiles = edges_ref.shape[0] // TILE
    lat_size = lax.axis_size("lat")
    lon = lax.axis_index("lon")
    lat = lax.axis_index("lat")
    twin = lon + 1 - 2 * lax.rem(lon, 2)
    across = lax.rem(lon + 2, 4)
    bands = [
        lat,
        lat + 1 - 2 * lax.rem(lat, 2),
        lax.rem(lat + 2, 4),
        3 - lat,
    ]
    lon_up, lon_down = lax.rem(lon + 1, 4), lax.rem(lon + 3, 4)
    lat_up, lat_down = lax.rem(lat + 1, 4), lax.rem(lat + 3, 4)

    barrier = pltpu.get_barrier_semaphore()
    partners = [(lon, bands[1]), (lon, bands[2]), (lon, bands[3]), (across, lat)]
    for side in (lon_up, lon_down):
        for band in (lat_down, lat, lat_up):
            partners.append((side, band))

    def edge_copy(t):
        rows = pl.ds(pl.multiple_of(t * TILE, TILE), TILE)
        return pltpu.make_async_copy(edges_ref.at[rows], edge_buf.at[rows], edge_sem.at[t])

    def message_copy(t):
        rows = pl.ds(pl.multiple_of(t * TILE, TILE), TILE)
        return pltpu.make_async_copy(message_buf.at[rows], message_ref.at[rows], message_sem.at[t])

    halo_base = nodes
    lat_base = nodes + 6 * RIM_LON
    recv_base = nodes + HALO
    table[pl.ds(nodes, HALO), :] = jnp.zeros((HALO, width), jnp.bfloat16)
    for other_lon, other_lat in partners:
        pl.semaphore_signal(
            barrier, inc=1, device_id={"lon": other_lon, "lat": other_lat}, device_id_type=MESH
        )
    for t in range(tiles):
        edge_copy(t).start()

    senders = (matmul(node_ref[...], edge_in_ref[pl.ds(width, width), :]) * 0.5).astype(jnp.bfloat16)
    table[pl.ds(0, nodes), :] = senders
    row_at = lax.broadcasted_iota(jnp.int32, (2 * RIM_LAT, nodes), 0)
    col_at = lax.broadcasted_iota(jnp.int32, (2 * RIM_LAT, nodes), 1)
    wanted = jnp.where(
        row_at < RIM_LAT, row_at * GRID_LAT, (row_at - RIM_LAT) * GRID_LAT + GRID_LAT - 1
    )
    picker = jnp.where(col_at == wanted, 1.0, 0.0).astype(jnp.bfloat16)
    rims[...] = matmul(picker, senders).astype(jnp.bfloat16)

    def remote(src, dst, send, recv, to_lon, to_lat):
        return pltpu.make_async_remote_copy(
            src_ref=src,
            dst_ref=dst,
            send_sem=send,
            recv_sem=recv,
            device_id={"lon": to_lon, "lat": to_lat},
            device_id_type=MESH,
        )

    halos = []
    for side, (to_lon, first) in enumerate(((lon_up, nodes - RIM_LON), (lon_down, 0))):
        for step, to_lat in enumerate((lat_up, lat, lat_down)):
            slot = side * 3 + step
            halos.append(
                remote(
                    table.at[pl.ds(first, RIM_LON)],
                    table.at[pl.ds(halo_base + slot * RIM_LON, RIM_LON)],
                    halo_send.at[slot],
                    halo_recv.at[slot],
                    to_lon,
                    to_lat,
                )
            )
    for side, (to_lat, first) in enumerate(((lat_up, RIM_LAT), (lat_down, 0))):
        slot = 6 + side
        halos.append(
            remote(
                rims.at[pl.ds(first, RIM_LAT)],
                table.at[pl.ds(lat_base + side * RIM_LAT, RIM_LAT)],
                halo_send.at[slot],
                halo_recv.at[slot],
                lon,
                to_lat,
            )
        )

    def block(owner_lon, owner_lat):
        at = (owner_lon * 4 + owner_lat) * GROUP
        return every_ref.at[pl.ds(pl.multiple_of(at, GROUP), GROUP)]

    def share(number, owner_lon, owner_lat, to_lon, to_lat):
        dst = block(owner_lon, owner_lat)
        src = table.at[pl.ds(0, GROUP)] if number < 5 else dst
        return remote(
            src, dst, send_sem.at[number], recv_sem.at[owner_lon * 4 + owner_lat], to_lon, to_lat
        )

    def arrived(owner_lon, owner_lat):
        share(5, owner_lon, owner_lat, twin, lat).wait_recv()

    own = [
        share(0, lon, lat, across, lat),
        share(1, lon, lat, lon, bands[1]),
        share(2, lon, lat, lon, bands[2]),
        share(3, lon, lat, lon, bands[3]),
        share(4, lon, lat, twin, lat),
    ]
    to_across = [None] + [share(4 + k, lon, bands[k], across, lat) for k in (1, 2, 3)]
    to_twin = [None] + [share(7 + k, lon, bands[k], twin, lat) for k in (1, 2, 3)]
    passed = [share(11 + k, across, bands[k], twin, lat) for k in (0, 1, 2, 3)]

    def from_band(k):
        arrived(lon, bands[k])
        to_across[k].start()
        to_twin[k].start()

    def from_across(k):
        arrived(across, bands[k])
        passed[k].start()

    pl.semaphore_wait(barrier, len(partners))
    for copy in halos:
        copy.start()
    for copy in own:
        copy.start()
    keep = pltpu.make_async_copy(table.at[pl.ds(0, GROUP)], block(lon, lat), own_sem)
    keep.start()

    receivers = (matmul(node_ref[...], edge_in_ref[pl.ds(2 * width, width), :]) * 0.5).astype(
        jnp.bfloat16
    )
    table[pl.ds(recv_base, nodes), :] = receivers
    recv_table_ref[...] = receivers
    edge_half[...] = edge_in_ref[pl.ds(0, width), :] * jnp.bfloat16(0.5)
    total_ref[...] = jnp.zeros_like(total_ref)

    source = lax.shift_right_logical(sender_ref[...], 9)
    row = lax.bitwise_and(sender_ref[...], 511)
    lon_shift = lax.bitwise_and(lax.shift_right_logical(source, 2) - lon + 4, 3)
    lat_shift = lax.bitwise_and(source, 3) - lat
    near_lon = (
        halo_base
        + (jnp.where(lon_shift == 3, 0, 3) + lat_shift + 1) * RIM_LON
        + lax.bitwise_and(row, GRID_LAT - 1)
    )
    near_lat = (
        lat_base
        + jnp.where(lat_shift == -1, 0, RIM_LAT)
        + lax.shift_right_logical(row, 4)
    )
    local = jnp.where(lon_shift != 0, near_lon, jnp.where(lat_shift != 0, near_lat, row))
    sender_ids[...] = local.astype(jnp.float32)
    receiver_ids[...] = receiver_ref[...].astype(jnp.float32)

    for copy in halos:
        copy.wait_recv()

    groups = TILE // GROUP
    per_sub = SUB // GROUP

    def tile(t, carry):
        @pl.when(t == 1)
        def _():
            from_band(1)

        @pl.when(t == 2)
        def _():
            from_band(2)
            from_across(0)

        @pl.when(t == 3)
        def _():
            from_band(3)
            from_across(1)

        @pl.when(t == 5)
        def _():
            from_across(2)

        edge_copy(t).wait()
        to_rows = []
        for part in range(TILE // SUB):
            first = t * TILE + part * SUB
            rows = pl.ds(pl.multiple_of(first, SUB), SUB)
            ids = [sender_ids[pl.ds(t * groups + part * per_sub + g, 1), :] for g in range(per_sub)]
            tos = [
                receiver_ids[pl.ds(t * groups + part * per_sub + g, 1), :] for g in range(per_sub)
            ]
            to_rows += tos
            picks = jnp.concatenate([one_hot(ids, nodes + HALO), one_hot(tos, nodes)], axis=1)
            half = matmul(edge_buf[rows, :], edge_half[...]) + matmul(picks, table[...])
            change = normed(matmul(silu_of_twice(half), edge_out_ref[...]), gain_ref[...])
            message_buf[rows, :] = change.astype(jnp.bfloat16)
        message_copy(t).start()
        spread = one_hot_across(to_rows, nodes)
        rows = pl.ds(pl.multiple_of(t * TILE, TILE), TILE)
        total_ref[...] += matmul(spread, message_buf[rows, :])
        return carry

    lax.fori_loop(0, tiles, tile, 0)
    from_across(3)
    for band in bands:
        arrived(twin, band)
        arrived(lax.rem(twin + 2, 4), band)
    for copy in halos + own + to_across[1:] + to_twin[1:] + passed:
        copy.wait_send()
    keep.wait()
    for t in range(tiles):
        message_copy(t).wait()


def last_kernel(
    fine_ref,
    message_ref,
    coarse_ref,
    sender_ref,
    receiver_ref,
    every_ref,
    recv_table_ref,
    total_ref,
    edge_in_ref,
    edge_out_ref,
    gain_ref,
    node_ref,
    node_in_ref,
    node_out_ref,
    node_gain_ref,
    fine_next_ref,
    coarse_next_ref,
    node_next_ref,
    total,
):
    step = pl.program_id(0)
    nodes, width = node_ref.shape

    @pl.when(step == 0)
    def _():
        total[...] = total_ref[...]

    fine_next_ref[...] = (
        fine_ref[...].astype(jnp.float32) + message_ref[...].astype(jnp.float32)
    ).astype(jnp.bfloat16)
    per = coarse_ref.shape[0] // GROUP
    ids = [sender_ref[pl.ds(step * per + g, 1), :].astype(jnp.float32) for g in range(per)]
    tos = [receiver_ref[pl.ds(step * per + g, 1), :].astype(jnp.float32) for g in range(per)]
    edges = coarse_ref[...]
    half = (
        matmul(edges, edge_in_ref[...]) * 0.5
        + matmul(one_hot(ids, every_ref.shape[0]), every_ref[...])
        + matmul(one_hot(tos, nodes), recv_table_ref[...])
    )
    change = normed(matmul(silu_of_twice(half), edge_out_ref[...]), gain_ref[...])
    coarse_next_ref[...] = (edges.astype(jnp.float32) + change).astype(jnp.bfloat16)
    total[...] += matmul(one_hot_across(tos, nodes), change.astype(jnp.bfloat16))

    @pl.when(step == pl.num_programs(0) - 1)
    def _():
        own = node_ref[...]
        inner = matmul(own, node_in_ref[pl.ds(0, width), :]) + matmul(
            total[...].astype(jnp.bfloat16), node_in_ref[pl.ds(width, width), :]
        )
        moved = normed(matmul(silu_of_twice(inner * 0.5), node_out_ref[...]), node_gain_ref[...])
        node_next_ref[...] = (own.astype(jnp.float32) + moved).astype(jnp.bfloat16)


def fast_shards(
    node_latent,
    fine_edges,
    coarse_edges,
    fine_sender,
    fine_receiver,
    coarse_peer,
    coarse_row,
    coarse_receiver,
    edge_in,
    edge_out,
    edge_gain,
    node_in,
    node_out,
    node_gain,
):
    nodes, width = node_latent.shape
    fine = fine_edges.shape[0]
    coarse = coarse_edges.shape[0]
    everyone = 16 * GROUP
    tiles = fine // TILE
    vmem = pl.BlockSpec(memory_space=pltpu.VMEM)
    hbm = pl.BlockSpec(memory_space=pl.ANY)
    table_rows = 2 * nodes + HALO
    dma = pltpu.SemaphoreType.DMA
    message, total, every, recv_table = pl.pallas_call(
        fine_kernel,
        out_shape=(
            jax.ShapeDtypeStruct((fine, width), jnp.bfloat16),
            jax.ShapeDtypeStruct((nodes, width), jnp.float32),
            jax.ShapeDtypeStruct((everyone, width), jnp.bfloat16),
            jax.ShapeDtypeStruct((nodes, width), jnp.bfloat16),
        ),
        in_specs=[vmem, hbm, vmem, vmem, vmem, vmem, vmem],
        out_specs=(hbm, vmem, hbm, vmem),
        scratch_shapes=[
            pltpu.VMEM((table_rows, width), jnp.bfloat16),
            pltpu.VMEM((2 * RIM_LAT, width), jnp.bfloat16),
            pltpu.VMEM((width, width), jnp.bfloat16),
            pltpu.VMEM((fine, width), jnp.bfloat16),
            pltpu.VMEM((fine, width), jnp.bfloat16),
            pltpu.VMEM((fine // GROUP, GROUP), jnp.float32),
            pltpu.VMEM((fine // GROUP, GROUP), jnp.float32),
            dma((tiles,)),
            dma((tiles,)),
            dma,
            dma((8,)),
            dma((8,)),
            dma((15,)),
            dma((16,)),
        ],
        compiler_params=pltpu.CompilerParams(
            collective_id=0, has_side_effects=True, vmem_limit_bytes=40 * 2**20
        ),
        cost_estimate=pl.CostEstimate(
            flops=10 * 10**9, bytes_accessed=12 * 2**20, transcendentals=fine * width
        ),
    )(
        node_latent,
        fine_edges,
        fine_sender.reshape(fine // GROUP, GROUP),
        fine_receiver.reshape(fine // GROUP, GROUP),
        edge_in,
        edge_out,
        edge_gain.reshape(1, width),
    )
    far = coarse_peer.reshape(coarse // GROUP, GROUP) * GROUP + coarse_row.reshape(
        coarse // GROUP, GROUP
    )
    steps = 4

    def rows_of(count):
        return pl.BlockSpec((count // steps, width), lambda i: (i, 0))

    def whole(shape):
        return pl.BlockSpec(shape, lambda i: (0, 0))

    fine_next, coarse_next, node_next = pl.pallas_call(
        last_kernel,
        grid=(steps,),
        out_shape=(
            jax.ShapeDtypeStruct((fine, width), jnp.bfloat16),
            jax.ShapeDtypeStruct((coarse, width), jnp.bfloat16),
            jax.ShapeDtypeStruct((nodes, width), jnp.bfloat16),
        ),
        in_specs=[
            rows_of(fine),
            rows_of(fine),
            rows_of(coarse),
            whole((coarse // GROUP, GROUP)),
            whole((coarse // GROUP, GROUP)),
            whole((everyone, width)),
            whole((nodes, width)),
            whole((nodes, width)),
            whole((width, width)),
            whole((width, width)),
            whole((1, width)),
            whole((nodes, width)),
            whole((2 * width, width)),
            whole((width, width)),
            whole((1, width)),
        ],
        out_specs=(rows_of(fine), rows_of(coarse), whole((nodes, width))),
        scratch_shapes=[pltpu.VMEM((nodes, width), jnp.float32)],
        compiler_params=pltpu.CompilerParams(vmem_limit_bytes=40 * 2**20),
        cost_estimate=pl.CostEstimate(
            flops=5 * 10**9, bytes_accessed=16 * 2**20, transcendentals=coarse * width
        ),
    )(
        fine_edges,
        message,
        coarse_edges,
        far,
        coarse_receiver.reshape(coarse // GROUP, GROUP),
        every,
        recv_table,
        total,
        edge_in,
        edge_out,
        edge_gain.reshape(1, width),
        node_latent,
        node_in,
        node_out,
        node_gain.reshape(1, width),
    )
    return (node_next, fine_next, coarse_next)


def with_halo(cells, sides, width, closed):
    for axis, dim in sides:
        count = lax.axis_size(axis)
        ends = count if closed else count - 1
        head = lax.slice_in_dim(cells, 0, width, axis=dim)
        tail = lax.slice_in_dim(cells, cells.shape[dim] - width, cells.shape[dim], axis=dim)
        cells = jnp.concatenate(
            [
                lax.ppermute(tail, axis, [(i, (i + 1) % count) for i in range(ends)]),
                cells,
                lax.ppermute(head, axis, [((i + 1) % count, i) for i in range(ends)]),
            ],
            axis=dim,
        )
    return cells


def layer_norm(values, gain):
    mean = jnp.mean(values, axis=-1, keepdims=True)
    centred = values - mean
    scale = lax.rsqrt(jnp.mean(centred * centred, axis=-1, keepdims=True) + 1e-05)
    return centred * scale * gain


def select_rows(table, picks):
    picker = (picks[:, None] == jnp.arange(table.shape[0], dtype=jnp.int32)[None, :]).astype(
        jnp.bfloat16
    )
    return jnp.dot(picker, table, preferred_element_type=jnp.float32).astype(jnp.bfloat16)


def shards(
    node_latent,
    fine_edges,
    coarse_edges,
    fine_sender,
    fine_receiver,
    coarse_peer,
    coarse_row,
    coarse_receiver,
    edge_in,
    edge_out,
    edge_gain,
    node_in,
    node_out,
    node_gain,
):
    node_count = node_latent.shape[0]
    width = node_latent.shape[1]
    coarse_count = node_count // 4
    fine_count = fine_edges.shape[0]
    lon_size = lax.axis_size("lon")
    lat_size = lax.axis_size("lat")
    lon_here = lax.axis_index("lon")
    lat_here = lax.axis_index("lat")
    grid_lon = node_count // GRID_LAT
    block = node_latent.reshape(grid_lon, GRID_LAT, width)
    sectors = with_halo(block, (("lon", 0),), 1, True)
    square = with_halo(sectors, (("lat", 1),), 1, False)
    beside_all = square.reshape((grid_lon + 2) * (GRID_LAT + 2), width)
    source = fine_sender // node_count
    row_index = fine_sender % node_count
    lon_shift = (source // lat_size - lon_here + 1 + lon_size) % lon_size - 1
    lat_shift = source % lat_size - lat_here
    place_i = row_index // GRID_LAT + 1 + lon_shift * grid_lon
    place_j = row_index % GRID_LAT + 1 + lat_shift * GRID_LAT
    local_sender = place_i * (GRID_LAT + 2) + place_j
    near = select_rows(beside_all, local_sender)
    peers = coarse_peer[:, 0]
    everyone = lax.all_gather(node_latent[:coarse_count], ("lon", "lat"), axis=0, tiled=True)
    far = jnp.take(everyone, peers * coarse_count + coarse_row, axis=0)
    targets = jnp.concatenate([fine_receiver, coarse_receiver], axis=0)
    edges = jnp.concatenate([fine_edges, coarse_edges], axis=0)
    senders = jnp.concatenate([near, far], axis=0)
    receivers = select_rows(node_latent, targets)
    joined = jnp.concatenate([edges, senders, receivers], axis=1)
    edge_hidden = jax.nn.silu(jnp.dot(joined, edge_in, preferred_element_type=jnp.float32)).astype(
        jnp.bfloat16
    )
    edge_change = layer_norm(
        jnp.dot(edge_hidden, edge_out, preferred_element_type=jnp.float32), edge_gain
    )
    message = edge_change.astype(jnp.bfloat16)
    edge_next = (edges.astype(jnp.float32) + edge_change).astype(jnp.bfloat16)
    selector = (jnp.arange(node_count, dtype=jnp.int32)[:, None] == targets[None, :]).astype(
        jnp.bfloat16
    )
    gathered = jnp.dot(selector, message, preferred_element_type=jnp.float32).astype(jnp.bfloat16)
    node_joined = jnp.concatenate([node_latent, gathered], axis=1)
    node_hidden = jax.nn.silu(
        jnp.dot(node_joined, node_in, preferred_element_type=jnp.float32)
    ).astype(jnp.bfloat16)
    node_change = layer_norm(
        jnp.dot(node_hidden, node_out, preferred_element_type=jnp.float32), node_gain
    )
    node_next = (node_latent.astype(jnp.float32) + node_change).astype(jnp.bfloat16)
    return (node_next, edge_next[:fine_count], edge_next[fine_count:])


def solution(mesh):
    small = mesh.shape["lon"] == 4 and mesh.shape["lat"] == 4
    return jax.shard_map(
        fast_shards if small else shards,
        mesh=mesh,
        in_specs=(
            P(("groups", "lon", "lat"), None),
            P(("groups", "lon", "lat"), None),
            P(("groups", "lon", "lat"), None),
            P(("groups", "lon", "lat")),
            P(("groups", "lon", "lat")),
            P(("groups", "lon", "lat"), None),
            P(("groups", "lon", "lat")),
            P(("groups", "lon", "lat")),
            P(),
            P(),
            P(),
            P(),
            P(),
            P(),
        ),
        out_specs=(
            P(("groups", "lon", "lat"), None),
            P(("groups", "lon", "lat"), None),
            P(("groups", "lon", "lat"), None),
        ),
        check_vma=False,
    )
```

```python
import jax
import jax.numpy as jnp
from jax import lax
from jax.experimental import pallas as pl
from jax.experimental.pallas import tpu as pltpu
from jax.sharding import PartitionSpec as P

GRID_LAT = 16
MESH = pl.DeviceIdType.MESH
GROUP = 128
TILE = 512
SUB = 512
LAST = 512
RIM_LON = 16
RIM_LAT = 32
HALO = 256


def one_hot(rows, width):
    lanes = lax.broadcasted_iota(jnp.int32, (GROUP, GROUP), 1).astype(jnp.float32)
    tall = []
    for row in rows:
        column = jnp.transpose(jnp.broadcast_to(row, (GROUP, GROUP)))
        tall.append(
            jnp.concatenate(
                [
                    jnp.where(column == lanes + float(first), 1.0, 0.0).astype(jnp.bfloat16)
                    for first in range(0, width, GROUP)
                ],
                axis=1,
            )
        )
    return jnp.concatenate(tall, axis=0)


def one_hot_across(rows, height):
    places = lax.broadcasted_iota(jnp.int32, (height, GROUP), 0).astype(jnp.float32)
    return jnp.concatenate(
        [jnp.where(places == row, 1.0, 0.0).astype(jnp.bfloat16) for row in rows], axis=1
    )


def matmul(a, b):
    return jnp.dot(a, b, preferred_element_type=jnp.float32)


def silu_of_twice(half):
    return (half * (1.0 + jnp.tanh(half))).astype(jnp.bfloat16)


def normed(values, gain):
    scale = 1.0 / values.shape[-1]
    mean = jnp.sum(values, axis=-1, keepdims=True) * scale
    centred = values - mean
    square = jnp.sum(centred * centred, axis=-1, keepdims=True) * scale
    return centred * lax.rsqrt(square + 1e-05) * gain


def fine_kernel(
    node_ref,
    edges_ref,
    sender_ref,
    receiver_ref,
    edge_in_ref,
    edge_out_ref,
    gain_ref,
    fine_next_ref,
    total_ref,
    every_ref,
    recv_table_ref,
    node,
    thirds,
    edge_out,
    gain,
    sender,
    receiver,
    table,
    rims,
    edge_half,
    edge_buf,
    sender_ids,
    receiver_ids,
    edge_sem,
    load_sem,
    own_sem,
    halo_send,
    halo_recv,
    send_sem,
    recv_sem,
):
    nodes, width = node_ref.shape
    tiles = edges_ref.shape[0] // TILE
    lat_size = lax.axis_size("lat")
    lon = lax.axis_index("lon")
    lat = lax.axis_index("lat")
    twin = lon + 1 - 2 * lax.rem(lon, 2)
    across = lax.rem(lon + 2, 4)
    bands = [
        lat,
        lat + 1 - 2 * lax.rem(lat, 2),
        lax.rem(lat + 2, 4),
        3 - lat,
    ]
    lon_up, lon_down = lax.rem(lon + 1, 4), lax.rem(lon + 3, 4)
    lat_up, lat_down = lax.rem(lat + 1, 4), lax.rem(lat + 3, 4)

    barrier = pltpu.get_barrier_semaphore()
    partners = [(lon, bands[1]), (lon, bands[2]), (lon, bands[3]), (across, lat)]
    for side in (lon_up, lon_down):
        for band in (lat_down, lat, lat_up):
            partners.append((side, band))

    def edge_copy(t):
        rows = pl.ds(pl.multiple_of(t * TILE, TILE), TILE)
        return pltpu.make_async_copy(edges_ref.at[rows], edge_buf.at[rows], edge_sem.at[t])

    def third(k):
        rows = pl.ds(k * width, width)
        return edge_in_ref.at[rows], thirds.at[rows]

    loads = [
        pltpu.make_async_copy(src, dst, load_sem.at[k])
        for k, (src, dst) in enumerate(
            (
                (node_ref, node),
                third(1),
                third(2),
                third(0),
                (sender_ref, sender),
                (receiver_ref, receiver),
                (edge_out_ref, edge_out),
                (gain_ref, gain),
            )
        )
    ]
    for load in loads[:2]:
        load.start()

    halo_base = nodes
    lat_base = nodes + 6 * RIM_LON
    recv_base = nodes + HALO
    table[pl.ds(nodes, HALO), :] = jnp.zeros((HALO, width), jnp.bfloat16)
    for other_lon, other_lat in partners:
        pl.semaphore_signal(
            barrier, inc=1, device_id={"lon": other_lon, "lat": other_lat}, device_id_type=MESH
        )
    for load in loads[2:]:
        load.start()
    for t in range(tiles):
        edge_copy(t).start()
    for load in loads[:2]:
        load.wait()

    senders = (matmul(node[...], thirds[pl.ds(width, width), :]) * 0.5).astype(jnp.bfloat16)
    table[pl.ds(0, nodes), :] = senders
    row_at = lax.broadcasted_iota(jnp.int32, (2 * RIM_LAT, nodes), 0)
    col_at = lax.broadcasted_iota(jnp.int32, (2 * RIM_LAT, nodes), 1)
    wanted = jnp.where(
        row_at < RIM_LAT, row_at * GRID_LAT, (row_at - RIM_LAT) * GRID_LAT + GRID_LAT - 1
    )
    picker = jnp.where(col_at == wanted, 1.0, 0.0).astype(jnp.bfloat16)
    rims[...] = matmul(picker, senders).astype(jnp.bfloat16)

    def remote(src, dst, send, recv, to_lon, to_lat):
        return pltpu.make_async_remote_copy(
            src_ref=src,
            dst_ref=dst,
            send_sem=send,
            recv_sem=recv,
            device_id={"lon": to_lon, "lat": to_lat},
            device_id_type=MESH,
        )

    halos = []
    for side, (to_lon, first) in enumerate(((lon_up, nodes - RIM_LON), (lon_down, 0))):
        for step, to_lat in enumerate((lat_up, lat, lat_down)):
            slot = side * 3 + step
            halos.append(
                remote(
                    table.at[pl.ds(first, RIM_LON)],
                    table.at[pl.ds(halo_base + slot * RIM_LON, RIM_LON)],
                    halo_send.at[slot],
                    halo_recv.at[slot],
                    to_lon,
                    to_lat,
                )
            )
    for side, (to_lat, first) in enumerate(((lat_up, RIM_LAT), (lat_down, 0))):
        slot = 6 + side
        halos.append(
            remote(
                rims.at[pl.ds(first, RIM_LAT)],
                table.at[pl.ds(lat_base + side * RIM_LAT, RIM_LAT)],
                halo_send.at[slot],
                halo_recv.at[slot],
                lon,
                to_lat,
            )
        )

    def block(owner_lon, owner_lat):
        at = (owner_lon * 4 + owner_lat) * GROUP
        return every_ref.at[pl.ds(pl.multiple_of(at, GROUP), GROUP)]

    def share(number, owner_lon, owner_lat, to_lon, to_lat):
        dst = block(owner_lon, owner_lat)
        src = table.at[pl.ds(0, GROUP)] if number < 5 else dst
        return remote(
            src, dst, send_sem.at[number], recv_sem.at[owner_lon * 4 + owner_lat], to_lon, to_lat
        )

    def arrived(owner_lon, owner_lat):
        share(5, owner_lon, owner_lat, twin, lat).wait_recv()

    own = [
        share(0, lon, lat, across, lat),
        share(1, lon, lat, lon, bands[1]),
        share(2, lon, lat, lon, bands[2]),
        share(3, lon, lat, lon, bands[3]),
        share(4, lon, lat, twin, lat),
    ]
    to_across = [None] + [share(4 + k, lon, bands[k], across, lat) for k in (1, 2, 3)]
    to_twin = [None] + [share(7 + k, lon, bands[k], twin, lat) for k in (1, 2, 3)]
    passed = [share(11 + k, across, bands[k], twin, lat) for k in (0, 1, 2, 3)]

    def from_band(k):
        arrived(lon, bands[k])
        to_across[k].start()
        to_twin[k].start()

    def from_across(k):
        arrived(across, bands[k])
        passed[k].start()

    pl.semaphore_wait(barrier, len(partners))
    for copy in halos:
        copy.start()
    for copy in own:
        copy.start()
    keep = pltpu.make_async_copy(table.at[pl.ds(0, GROUP)], block(lon, lat), own_sem)
    keep.start()

    for load in loads[2:]:
        load.wait()
    receivers = (matmul(node[...], thirds[pl.ds(2 * width, width), :]) * 0.5).astype(
        jnp.bfloat16
    )
    table[pl.ds(recv_base, nodes), :] = receivers
    recv_table_ref[...] = receivers
    edge_half[...] = thirds[pl.ds(0, width), :] * jnp.bfloat16(0.5)
    total_ref[...] = jnp.zeros_like(total_ref)

    source = lax.shift_right_logical(sender[...], 9)
    row = lax.bitwise_and(sender[...], 511)
    lon_shift = lax.bitwise_and(lax.shift_right_logical(source, 2) - lon + 4, 3)
    lat_shift = lax.bitwise_and(source, 3) - lat
    near_lon = (
        halo_base
        + (jnp.where(lon_shift == 3, 0, 3) + lat_shift + 1) * RIM_LON
        + lax.bitwise_and(row, GRID_LAT - 1)
    )
    near_lat = (
        lat_base
        + jnp.where(lat_shift == -1, 0, RIM_LAT)
        + lax.shift_right_logical(row, 4)
    )
    local = jnp.where(lon_shift != 0, near_lon, jnp.where(lat_shift != 0, near_lat, row))
    sender_ids[...] = local.astype(jnp.float32)
    receiver_ids[...] = receiver[...].astype(jnp.float32)

    for copy in halos:
        copy.wait_recv()

    groups = TILE // GROUP
    per_sub = SUB // GROUP

    def tile(t, carry):
        @pl.when(t == 1)
        def _():
            from_band(1)

        @pl.when(t == 2)
        def _():
            from_band(2)
            from_across(0)

        @pl.when(t == 3)
        def _():
            from_band(3)
            from_across(1)

        @pl.when(t == 5)
        def _():
            from_across(2)

        edge_copy(t).wait()
        to_rows, messages = [], []
        for part in range(TILE // SUB):
            first = t * TILE + part * SUB
            rows = pl.ds(pl.multiple_of(first, SUB), SUB)
            ids = [sender_ids[pl.ds(t * groups + part * per_sub + g, 1), :] for g in range(per_sub)]
            tos = [
                receiver_ids[pl.ds(t * groups + part * per_sub + g, 1), :] for g in range(per_sub)
            ]
            to_rows += tos
            picks = jnp.concatenate([one_hot(ids, nodes + HALO), one_hot(tos, nodes)], axis=1)
            edges = edge_buf[rows, :]
            half = matmul(edges, edge_half[...]) + matmul(picks, table[...])
            change = normed(matmul(silu_of_twice(half), edge_out[...]), gain[...])
            fine_next_ref[rows, :] = (edges.astype(jnp.float32) + change).astype(jnp.bfloat16)
            messages.append(change.astype(jnp.bfloat16))
        spread = one_hot_across(to_rows, nodes)
        total_ref[...] += matmul(spread, jnp.concatenate(messages, axis=0))
        return carry

    lax.fori_loop(0, tiles, tile, 0)
    from_across(3)
    for band in bands:
        arrived(twin, band)
        arrived(lax.rem(twin + 2, 4), band)
    for copy in halos + own + to_across[1:] + to_twin[1:] + passed:
        copy.wait_send()
    keep.wait()


def last_kernel(
    fine_ref,
    coarse_ref,
    peer_ref,
    row_ref,
    receiver_ref,
    every_ref,
    recv_table_ref,
    total_ref,
    edge_in_ref,
    edge_out_ref,
    gain_ref,
    node_ref,
    node_in_ref,
    node_out_ref,
    node_gain_ref,
    fine_next_ref,
    coarse_next_ref,
    node_next_ref,
    coarse_buf,
    out_sem,
):
    nodes, width = node_ref.shape
    count = coarse_ref.shape[0]
    fine_out = pltpu.make_async_copy(fine_ref, fine_next_ref, out_sem.at[0])
    fine_out.start()
    far = (peer_ref[...] * GROUP + row_ref[...]).astype(jnp.float32)
    to = receiver_ref[...].astype(jnp.float32)
    per = LAST // GROUP
    outs = [fine_out]
    total = total_ref[...]
    for part in range(count // LAST):
        ids = [far[part * per + g : part * per + g + 1, :] for g in range(per)]
        tos = [to[part * per + g : part * per + g + 1, :] for g in range(per)]
        rows = pl.ds(part * LAST, LAST)
        edges = coarse_ref[rows, :]
        half = (
            matmul(edges, edge_in_ref[pl.ds(0, width), :]) * 0.5
            + matmul(one_hot(ids, every_ref.shape[0]), every_ref[...])
            + matmul(one_hot(tos, nodes), recv_table_ref[...])
        )
        change = normed(matmul(silu_of_twice(half), edge_out_ref[...]), gain_ref[...])
        coarse_buf[rows, :] = (edges.astype(jnp.float32) + change).astype(jnp.bfloat16)
        out = pltpu.make_async_copy(
            coarse_buf.at[rows], coarse_next_ref.at[rows], out_sem.at[part + 1]
        )
        out.start()
        outs.append(out)
        total = total + matmul(one_hot_across(tos, nodes), change.astype(jnp.bfloat16))
    own = node_ref[...]
    inner = matmul(own, node_in_ref[pl.ds(0, width), :]) + matmul(
        total.astype(jnp.bfloat16), node_in_ref[pl.ds(width, width), :]
    )
    moved = normed(matmul(silu_of_twice(inner * 0.5), node_out_ref[...]), node_gain_ref[...])
    node_next_ref[...] = (own.astype(jnp.float32) + moved).astype(jnp.bfloat16)
    for out in outs:
        out.wait()


def fast_shards(
    node_latent,
    fine_edges,
    coarse_edges,
    fine_sender,
    fine_receiver,
    coarse_peer,
    coarse_row,
    coarse_receiver,
    edge_in,
    edge_out,
    edge_gain,
    node_in,
    node_out,
    node_gain,
):
    nodes, width = node_latent.shape
    fine = fine_edges.shape[0]
    coarse = coarse_edges.shape[0]
    everyone = 16 * GROUP
    tiles = fine // TILE
    vmem = pl.BlockSpec(memory_space=pltpu.VMEM)
    hbm = pl.BlockSpec(memory_space=pltpu.HBM)
    table_rows = 2 * nodes + HALO
    dma = pltpu.SemaphoreType.DMA
    fine_made, total, every, recv_table = pl.pallas_call(
        fine_kernel,
        out_shape=(
            jax.ShapeDtypeStruct((fine, width), jnp.bfloat16),
            jax.ShapeDtypeStruct((nodes, width), jnp.float32),
            jax.ShapeDtypeStruct((everyone, width), jnp.bfloat16),
            jax.ShapeDtypeStruct((nodes, width), jnp.bfloat16),
        ),
        in_specs=[hbm] * 7,
        out_specs=(vmem,) * 4,
        scratch_shapes=[
            pltpu.VMEM((nodes, width), jnp.bfloat16),
            pltpu.VMEM((3 * width, width), jnp.bfloat16),
            pltpu.VMEM((width, width), jnp.bfloat16),
            pltpu.VMEM((1, width), jnp.float32),
            pltpu.VMEM((fine // GROUP, GROUP), jnp.int32),
            pltpu.VMEM((fine // GROUP, GROUP), jnp.int32),
            pltpu.VMEM((table_rows, width), jnp.bfloat16),
            pltpu.VMEM((2 * RIM_LAT, width), jnp.bfloat16),
            pltpu.VMEM((width, width), jnp.bfloat16),
            pltpu.VMEM((fine, width), jnp.bfloat16),
            pltpu.VMEM((fine // GROUP, GROUP), jnp.float32),
            pltpu.VMEM((fine // GROUP, GROUP), jnp.float32),
            dma((tiles,)),
            dma((8,)),
            dma,
            dma((8,)),
            dma((8,)),
            dma((15,)),
            dma((16,)),
        ],
        compiler_params=pltpu.CompilerParams(
            collective_id=0, has_side_effects=True, vmem_limit_bytes=36 * 2**20
        ),
        cost_estimate=pl.CostEstimate(
            flops=10 * 10**9, bytes_accessed=12 * 2**20, transcendentals=fine * width
        ),
    )(
        *[
            pltpu.with_memory_space_constraint(operand, pltpu.HBM)
            for operand in (
                node_latent,
                fine_edges,
                fine_sender.reshape(fine // GROUP, GROUP),
                fine_receiver.reshape(fine // GROUP, GROUP),
                edge_in,
                edge_out,
                edge_gain.reshape(1, width),
            )
        ]
    )
    fine_next, coarse_next, node_next = pl.pallas_call(
        last_kernel,
        out_shape=(
            jax.ShapeDtypeStruct((fine, width), jnp.bfloat16),
            jax.ShapeDtypeStruct((coarse, width), jnp.bfloat16),
            jax.ShapeDtypeStruct((nodes, width), jnp.bfloat16),
        ),
        in_specs=[vmem] * 15,
        out_specs=(hbm, hbm, vmem),
        scratch_shapes=[
            pltpu.VMEM((coarse, width), jnp.bfloat16),
            dma((1 + coarse // LAST,)),
        ],
        compiler_params=pltpu.CompilerParams(vmem_limit_bytes=36 * 2**20),
        cost_estimate=pl.CostEstimate(
            flops=5 * 10**9, bytes_accessed=16 * 2**20, transcendentals=coarse * width
        ),
    )(
        fine_made,
        coarse_edges,
        coarse_peer.reshape(coarse // GROUP, GROUP),
        coarse_row.reshape(coarse // GROUP, GROUP),
        coarse_receiver.reshape(coarse // GROUP, GROUP),
        every,
        recv_table,
        total,
        edge_in,
        edge_out,
        edge_gain.reshape(1, width),
        node_latent,
        node_in,
        node_out,
        node_gain.reshape(1, width),
    )
    return (node_next, fine_next, coarse_next)


def with_halo(cells, sides, width, closed):
    for axis, dim in sides:
        count = lax.axis_size(axis)
        ends = count if closed else count - 1
        head = lax.slice_in_dim(cells, 0, width, axis=dim)
        tail = lax.slice_in_dim(cells, cells.shape[dim] - width, cells.shape[dim], axis=dim)
        cells = jnp.concatenate(
            [
                lax.ppermute(tail, axis, [(i, (i + 1) % count) for i in range(ends)]),
                cells,
                lax.ppermute(head, axis, [((i + 1) % count, i) for i in range(ends)]),
            ],
            axis=dim,
        )
    return cells


def layer_norm(values, gain):
    mean = jnp.mean(values, axis=-1, keepdims=True)
    centred = values - mean
    scale = lax.rsqrt(jnp.mean(centred * centred, axis=-1, keepdims=True) + 1e-05)
    return centred * scale * gain


def select_rows(table, picks):
    picker = (picks[:, None] == jnp.arange(table.shape[0], dtype=jnp.int32)[None, :]).astype(
        jnp.bfloat16
    )
    return jnp.dot(picker, table, preferred_element_type=jnp.float32).astype(jnp.bfloat16)


def shards(
    node_latent,
    fine_edges,
    coarse_edges,
    fine_sender,
    fine_receiver,
    coarse_peer,
    coarse_row,
    coarse_receiver,
    edge_in,
    edge_out,
    edge_gain,
    node_in,
    node_out,
    node_gain,
):
    node_count = node_latent.shape[0]
    width = node_latent.shape[1]
    coarse_count = node_count // 4
    fine_count = fine_edges.shape[0]
    lon_size = lax.axis_size("lon")
    lat_size = lax.axis_size("lat")
    lon_here = lax.axis_index("lon")
    lat_here = lax.axis_index("lat")
    grid_lon = node_count // GRID_LAT
    block = node_latent.reshape(grid_lon, GRID_LAT, width)
    sectors = with_halo(block, (("lon", 0),), 1, True)
    square = with_halo(sectors, (("lat", 1),), 1, False)
    beside_all = square.reshape((grid_lon + 2) * (GRID_LAT + 2), width)
    source = fine_sender // node_count
    row_index = fine_sender % node_count
    lon_shift = (source // lat_size - lon_here + 1 + lon_size) % lon_size - 1
    lat_shift = source % lat_size - lat_here
    place_i = row_index // GRID_LAT + 1 + lon_shift * grid_lon
    place_j = row_index % GRID_LAT + 1 + lat_shift * GRID_LAT
    local_sender = place_i * (GRID_LAT + 2) + place_j
    near = select_rows(beside_all, local_sender)
    peers = coarse_peer[:, 0]
    everyone = lax.all_gather(node_latent[:coarse_count], ("lon", "lat"), axis=0, tiled=True)
    far = jnp.take(everyone, peers * coarse_count + coarse_row, axis=0)
    targets = jnp.concatenate([fine_receiver, coarse_receiver], axis=0)
    edges = jnp.concatenate([fine_edges, coarse_edges], axis=0)
    senders = jnp.concatenate([near, far], axis=0)
    receivers = select_rows(node_latent, targets)
    joined = jnp.concatenate([edges, senders, receivers], axis=1)
    edge_hidden = jax.nn.silu(jnp.dot(joined, edge_in, preferred_element_type=jnp.float32)).astype(
        jnp.bfloat16
    )
    edge_change = layer_norm(
        jnp.dot(edge_hidden, edge_out, preferred_element_type=jnp.float32), edge_gain
    )
    message = edge_change.astype(jnp.bfloat16)
    edge_next = (edges.astype(jnp.float32) + edge_change).astype(jnp.bfloat16)
    selector = (jnp.arange(node_count, dtype=jnp.int32)[:, None] == targets[None, :]).astype(
        jnp.bfloat16
    )
    gathered = jnp.dot(selector, message, preferred_element_type=jnp.float32).astype(jnp.bfloat16)
    node_joined = jnp.concatenate([node_latent, gathered], axis=1)
    node_hidden = jax.nn.silu(
        jnp.dot(node_joined, node_in, preferred_element_type=jnp.float32)
    ).astype(jnp.bfloat16)
    node_change = layer_norm(
        jnp.dot(node_hidden, node_out, preferred_element_type=jnp.float32), node_gain
    )
    node_next = (node_latent.astype(jnp.float32) + node_change).astype(jnp.bfloat16)
    return (node_next, edge_next[:fine_count], edge_next[fine_count:])


def solution(mesh):
    small = mesh.shape["lon"] == 4 and mesh.shape["lat"] == 4
    return jax.shard_map(
        fast_shards if small else shards,
        mesh=mesh,
        in_specs=(
            P(("groups", "lon", "lat"), None),
            P(("groups", "lon", "lat"), None),
            P(("groups", "lon", "lat"), None),
            P(("groups", "lon", "lat")),
            P(("groups", "lon", "lat")),
            P(("groups", "lon", "lat"), None),
            P(("groups", "lon", "lat")),
            P(("groups", "lon", "lat")),
            P(),
            P(),
            P(),
            P(),
            P(),
            P(),
        ),
        out_specs=(
            P(("groups", "lon", "lat"), None),
            P(("groups", "lon", "lat"), None),
            P(("groups", "lon", "lat"), None),
        ),
        check_vma=False,
    )
```

```python
import jax
import jax.numpy as jnp
from jax import lax
from jax.experimental import pallas as pl
from jax.experimental.pallas import tpu as pltpu
from jax.sharding import PartitionSpec as P

GRID_LAT = 16
MESH = pl.DeviceIdType.MESH
GROUP = 128
TILE = 512
SUB = 512
LAST = 512
RIM_LON = 16
RIM_LAT = 32
HALO = 256


def one_hot(rows, width):
    lanes = lax.broadcasted_iota(jnp.int32, (GROUP, GROUP), 1).astype(jnp.float32)
    tall = []
    for row in rows:
        column = jnp.transpose(jnp.broadcast_to(row, (GROUP, GROUP)))
        tall.append(
            jnp.concatenate(
                [
                    jnp.where(column == lanes + float(first), 1.0, 0.0).astype(jnp.bfloat16)
                    for first in range(0, width, GROUP)
                ],
                axis=1,
            )
        )
    return jnp.concatenate(tall, axis=0)


def one_hot_across(rows, height):
    places = lax.broadcasted_iota(jnp.int32, (height, GROUP), 0).astype(jnp.float32)
    return jnp.concatenate(
        [jnp.where(places == row, 1.0, 0.0).astype(jnp.bfloat16) for row in rows], axis=1
    )


def matmul(a, b):
    return jnp.dot(a, b, preferred_element_type=jnp.float32)


def silu_of_twice(half):
    return (half * (1.0 + jnp.tanh(half))).astype(jnp.bfloat16)


def normed(values, gain):
    scale = 1.0 / values.shape[-1]
    mean = jnp.sum(values, axis=-1, keepdims=True) * scale
    centred = values - mean
    square = jnp.sum(centred * centred, axis=-1, keepdims=True) * scale
    return centred * lax.rsqrt(square + 1e-05) * gain


def fine_kernel(
    node_ref,
    edges_ref,
    sender_ref,
    receiver_ref,
    edge_in_ref,
    edge_out_ref,
    gain_ref,
    coarse_ref,
    coarse_to_ref,
    fine_next_ref,
    total_ref,
    every_ref,
    coarse_base_ref,
    node,
    thirds,
    edge_out,
    gain,
    sender,
    receiver,
    table,
    rims,
    edge_half,
    edge_buf,
    base,
    coarse_buf,
    coarse_to,
    sender_ids,
    receiver_ids,
    edge_sem,
    load_sem,
    own_sem,
    halo_send,
    halo_recv,
    send_sem,
    recv_sem,
):
    nodes, width = node_ref.shape
    tiles = edges_ref.shape[0] // TILE
    lat_size = lax.axis_size("lat")
    lon = lax.axis_index("lon")
    lat = lax.axis_index("lat")
    twin = lon + 1 - 2 * lax.rem(lon, 2)
    across = lax.rem(lon + 2, 4)
    bands = [
        lat,
        lat + 1 - 2 * lax.rem(lat, 2),
        lax.rem(lat + 2, 4),
        3 - lat,
    ]
    lon_up, lon_down = lax.rem(lon + 1, 4), lax.rem(lon + 3, 4)
    lat_up, lat_down = lax.rem(lat + 1, 4), lax.rem(lat + 3, 4)

    barrier = pltpu.get_barrier_semaphore()
    partners = [(lon, bands[1]), (lon, bands[2]), (lon, bands[3]), (across, lat)]
    for side in (lon_up, lon_down):
        for band in (lat_down, lat, lat_up):
            partners.append((side, band))

    def edge_copy(t):
        rows = pl.ds(pl.multiple_of(t * TILE, TILE), TILE)
        return pltpu.make_async_copy(edges_ref.at[rows], edge_buf.at[rows], edge_sem.at[t])

    def third(k):
        rows = pl.ds(k * width, width)
        return edge_in_ref.at[rows], thirds.at[rows]

    loads = [
        pltpu.make_async_copy(src, dst, load_sem.at[k])
        for k, (src, dst) in enumerate(
            (
                (node_ref, node),
                third(1),
                third(2),
                third(0),
                (sender_ref, sender),
                (receiver_ref, receiver),
                (edge_out_ref, edge_out),
                (gain_ref, gain),
                (coarse_ref, coarse_buf),
                (coarse_to_ref, coarse_to),
            )
        )
    ]
    for load in loads[:2]:
        load.start()

    halo_base = nodes
    lat_base = nodes + 6 * RIM_LON
    recv_base = nodes + HALO
    table[pl.ds(nodes, HALO), :] = jnp.zeros((HALO, width), jnp.bfloat16)
    for other_lon, other_lat in partners:
        pl.semaphore_signal(
            barrier, inc=1, device_id={"lon": other_lon, "lat": other_lat}, device_id_type=MESH
        )
    for load in loads[2:8]:
        load.start()
    for t in range(tiles):
        edge_copy(t).start()
    for load in loads[8:]:
        load.start()
    for load in loads[:2]:
        load.wait()

    senders = (matmul(node[...], thirds[pl.ds(width, width), :]) * 0.5).astype(jnp.bfloat16)
    table[pl.ds(0, nodes), :] = senders
    row_at = lax.broadcasted_iota(jnp.int32, (2 * RIM_LAT, nodes), 0)
    col_at = lax.broadcasted_iota(jnp.int32, (2 * RIM_LAT, nodes), 1)
    wanted = jnp.where(
        row_at < RIM_LAT, row_at * GRID_LAT, (row_at - RIM_LAT) * GRID_LAT + GRID_LAT - 1
    )
    picker = jnp.where(col_at == wanted, 1.0, 0.0).astype(jnp.bfloat16)
    rims[...] = matmul(picker, senders).astype(jnp.bfloat16)

    def remote(src, dst, send, recv, to_lon, to_lat):
        return pltpu.make_async_remote_copy(
            src_ref=src,
            dst_ref=dst,
            send_sem=send,
            recv_sem=recv,
            device_id={"lon": to_lon, "lat": to_lat},
            device_id_type=MESH,
        )

    halos = []
    for side, (to_lon, first) in enumerate(((lon_up, nodes - RIM_LON), (lon_down, 0))):
        for step, to_lat in enumerate((lat_up, lat, lat_down)):
            slot = side * 3 + step
            halos.append(
                remote(
                    table.at[pl.ds(first, RIM_LON)],
                    table.at[pl.ds(halo_base + slot * RIM_LON, RIM_LON)],
                    halo_send.at[slot],
                    halo_recv.at[slot],
                    to_lon,
                    to_lat,
                )
            )
    for side, (to_lat, first) in enumerate(((lat_up, RIM_LAT), (lat_down, 0))):
        slot = 6 + side
        halos.append(
            remote(
                rims.at[pl.ds(first, RIM_LAT)],
                table.at[pl.ds(lat_base + side * RIM_LAT, RIM_LAT)],
                halo_send.at[slot],
                halo_recv.at[slot],
                lon,
                to_lat,
            )
        )

    def block(owner_lon, owner_lat):
        at = (owner_lon * 4 + owner_lat) * GROUP
        return every_ref.at[pl.ds(pl.multiple_of(at, GROUP), GROUP)]

    def share(number, owner_lon, owner_lat, to_lon, to_lat):
        dst = block(owner_lon, owner_lat)
        src = table.at[pl.ds(0, GROUP)] if number < 5 else dst
        return remote(
            src, dst, send_sem.at[number], recv_sem.at[owner_lon * 4 + owner_lat], to_lon, to_lat
        )

    def arrived(owner_lon, owner_lat):
        share(5, owner_lon, owner_lat, twin, lat).wait_recv()

    own = [
        share(0, lon, lat, across, lat),
        share(1, lon, lat, lon, bands[1]),
        share(2, lon, lat, lon, bands[2]),
        share(3, lon, lat, lon, bands[3]),
        share(4, lon, lat, twin, lat),
    ]
    to_across = [None] + [share(4 + k, lon, bands[k], across, lat) for k in (1, 2, 3)]
    to_twin = [None] + [share(7 + k, lon, bands[k], twin, lat) for k in (1, 2, 3)]
    passed = [share(11 + k, across, bands[k], twin, lat) for k in (0, 1, 2, 3)]

    def from_band(k):
        arrived(lon, bands[k])
        to_across[k].start()
        to_twin[k].start()

    def from_across(k):
        arrived(across, bands[k])
        passed[k].start()

    pl.semaphore_wait(barrier, len(partners))
    own[0].start()
    for copy in halos:
        copy.start()
    for copy in own[1:]:
        copy.start()
    keep = pltpu.make_async_copy(table.at[pl.ds(0, GROUP)], block(lon, lat), own_sem)
    keep.start()

    for load in loads[2:8]:
        load.wait()
    receivers = (matmul(node[...], thirds[pl.ds(2 * width, width), :]) * 0.5).astype(
        jnp.bfloat16
    )
    table[pl.ds(recv_base, nodes), :] = receivers
    edge_half[...] = thirds[pl.ds(0, width), :] * jnp.bfloat16(0.5)
    total_ref[...] = jnp.zeros_like(total_ref)

    source = lax.shift_right_logical(sender[...], 9)
    row = lax.bitwise_and(sender[...], 511)
    lon_shift = lax.bitwise_and(lax.shift_right_logical(source, 2) - lon + 4, 3)
    lat_shift = lax.bitwise_and(source, 3) - lat
    near_lon = (
        halo_base
        + (jnp.where(lon_shift == 3, 0, 3) + lat_shift + 1) * RIM_LON
        + lax.bitwise_and(row, GRID_LAT - 1)
    )
    near_lat = (
        lat_base
        + jnp.where(lat_shift == -1, 0, RIM_LAT)
        + lax.shift_right_logical(row, 4)
    )
    local = jnp.where(lon_shift != 0, near_lon, jnp.where(lat_shift != 0, near_lat, row))
    sender_ids[...] = local.astype(jnp.float32)
    receiver_ids[...] = receiver[...].astype(jnp.float32)

    groups = TILE // GROUP
    per_sub = SUB // GROUP

    def base_tile(t, carry):
        edge_copy(t).wait()
        rows = pl.ds(pl.multiple_of(t * TILE, TILE), TILE)
        tos = [receiver_ids[pl.ds(t * groups + g, 1), :] for g in range(groups)]
        base[rows, :] = matmul(edge_buf[rows, :], edge_half[...]) + matmul(
            one_hot(tos, nodes), table[pl.ds(recv_base, nodes), :]
        )
        return carry

    lax.fori_loop(0, tiles, base_tile, 0)
    for copy in halos:
        copy.wait_recv()

    def tile(t, carry):
        @pl.when(t == 1)
        def _():
            from_band(1)
            from_across(0)

        @pl.when(t == 3)
        def _():
            from_band(2)

        @pl.when(t == 5)
        def _():
            from_band(3)
            from_across(1)

        to_rows, messages = [], []
        for part in range(TILE // SUB):
            first = t * TILE + part * SUB
            rows = pl.ds(pl.multiple_of(first, SUB), SUB)
            ids = [sender_ids[pl.ds(t * groups + part * per_sub + g, 1), :] for g in range(per_sub)]
            tos = [
                receiver_ids[pl.ds(t * groups + part * per_sub + g, 1), :] for g in range(per_sub)
            ]
            to_rows += tos
            edges = edge_buf[rows, :]
            half = base[rows, :] + matmul(
                one_hot(ids, nodes + HALO), table[pl.ds(0, nodes + HALO), :]
            )
            change = normed(matmul(silu_of_twice(half), edge_out[...]), gain[...])
            fine_next_ref[rows, :] = (edges.astype(jnp.float32) + change).astype(jnp.bfloat16)
            messages.append(change.astype(jnp.bfloat16))
        spread = one_hot_across(to_rows, nodes)
        total_ref[...] += matmul(spread, jnp.concatenate(messages, axis=0))
        return carry

    lax.fori_loop(0, tiles, tile, 0)
    from_across(2)
    for load in loads[8:]:
        load.wait()
    coarse_tos = coarse_to[...].astype(jnp.float32)
    for part in range(coarse_buf.shape[0] // LAST):
        rows = pl.ds(part * LAST, LAST)
        first = part * (LAST // GROUP)
        tos = [coarse_tos[first + g : first + g + 1, :] for g in range(LAST // GROUP)]
        coarse_base_ref[rows, :] = matmul(coarse_buf[rows, :], edge_half[...]) + matmul(
            one_hot(tos, nodes), table[pl.ds(recv_base, nodes), :]
        )
    from_across(3)
    for band in bands:
        arrived(twin, band)
        arrived(lax.rem(twin + 2, 4), band)
    for copy in halos + own + to_across[1:] + to_twin[1:] + passed:
        copy.wait_send()
    keep.wait()


def last_kernel(
    fine_ref,
    coarse_ref,
    peer_ref,
    row_ref,
    receiver_ref,
    every_ref,
    coarse_base_ref,
    total_ref,
    edge_out_ref,
    gain_ref,
    node_ref,
    node_in_ref,
    node_out_ref,
    node_gain_ref,
    fine_next_ref,
    coarse_next_ref,
    node_next_ref,
    coarse_buf,
    out_sem,
):
    nodes, width = node_ref.shape
    count = coarse_ref.shape[0]
    fine_out = pltpu.make_async_copy(fine_ref, fine_next_ref, out_sem.at[0])
    fine_out.start()
    far = (peer_ref[...] * GROUP + row_ref[...]).astype(jnp.float32)
    to = receiver_ref[...].astype(jnp.float32)
    per = LAST // GROUP
    outs = [fine_out]
    total = total_ref[...]
    for part in range(count // LAST):
        ids = [far[part * per + g : part * per + g + 1, :] for g in range(per)]
        tos = [to[part * per + g : part * per + g + 1, :] for g in range(per)]
        rows = pl.ds(part * LAST, LAST)
        edges = coarse_ref[rows, :]
        half = coarse_base_ref[rows, :] + matmul(
            one_hot(ids, every_ref.shape[0]), every_ref[...]
        )
        change = normed(matmul(silu_of_twice(half), edge_out_ref[...]), gain_ref[...])
        coarse_buf[rows, :] = (edges.astype(jnp.float32) + change).astype(jnp.bfloat16)
        out = pltpu.make_async_copy(
            coarse_buf.at[rows], coarse_next_ref.at[rows], out_sem.at[part + 1]
        )
        out.start()
        outs.append(out)
        total = total + matmul(one_hot_across(tos, nodes), change.astype(jnp.bfloat16))
    own = node_ref[...]
    inner = matmul(own, node_in_ref[pl.ds(0, width), :]) + matmul(
        total.astype(jnp.bfloat16), node_in_ref[pl.ds(width, width), :]
    )
    moved = normed(matmul(silu_of_twice(inner * 0.5), node_out_ref[...]), node_gain_ref[...])
    node_next_ref[...] = (own.astype(jnp.float32) + moved).astype(jnp.bfloat16)
    for out in outs:
        out.wait()


def fast_shards(
    node_latent,
    fine_edges,
    coarse_edges,
    fine_sender,
    fine_receiver,
    coarse_peer,
    coarse_row,
    coarse_receiver,
    edge_in,
    edge_out,
    edge_gain,
    node_in,
    node_out,
    node_gain,
):
    nodes, width = node_latent.shape
    fine = fine_edges.shape[0]
    coarse = coarse_edges.shape[0]
    everyone = 16 * GROUP
    tiles = fine // TILE
    vmem = pl.BlockSpec(memory_space=pltpu.VMEM)
    hbm = pl.BlockSpec(memory_space=pltpu.HBM)
    table_rows = 2 * nodes + HALO
    dma = pltpu.SemaphoreType.DMA
    fine_made, total, every, coarse_base = pl.pallas_call(
        fine_kernel,
        out_shape=(
            jax.ShapeDtypeStruct((fine, width), jnp.bfloat16),
            jax.ShapeDtypeStruct((nodes, width), jnp.float32),
            jax.ShapeDtypeStruct((everyone, width), jnp.bfloat16),
            jax.ShapeDtypeStruct((coarse, width), jnp.float32),
        ),
        in_specs=[hbm] * 9,
        out_specs=(vmem,) * 4,
        scratch_shapes=[
            pltpu.VMEM((nodes, width), jnp.bfloat16),
            pltpu.VMEM((3 * width, width), jnp.bfloat16),
            pltpu.VMEM((width, width), jnp.bfloat16),
            pltpu.VMEM((1, width), jnp.float32),
            pltpu.VMEM((fine // GROUP, GROUP), jnp.int32),
            pltpu.VMEM((fine // GROUP, GROUP), jnp.int32),
            pltpu.VMEM((table_rows, width), jnp.bfloat16),
            pltpu.VMEM((2 * RIM_LAT, width), jnp.bfloat16),
            pltpu.VMEM((width, width), jnp.bfloat16),
            pltpu.VMEM((fine, width), jnp.bfloat16),
            pltpu.VMEM((fine, width), jnp.float32),
            pltpu.VMEM((coarse, width), jnp.bfloat16),
            pltpu.VMEM((coarse // GROUP, GROUP), jnp.int32),
            pltpu.VMEM((fine // GROUP, GROUP), jnp.float32),
            pltpu.VMEM((fine // GROUP, GROUP), jnp.float32),
            dma((tiles,)),
            dma((10,)),
            dma,
            dma((8,)),
            dma((8,)),
            dma((15,)),
            dma((16,)),
        ],
        compiler_params=pltpu.CompilerParams(
            collective_id=0, has_side_effects=True, vmem_limit_bytes=36 * 2**20
        ),
        cost_estimate=pl.CostEstimate(
            flops=10 * 10**9, bytes_accessed=12 * 2**20, transcendentals=fine * width
        ),
    )(
        *[
            pltpu.with_memory_space_constraint(operand, pltpu.HBM)
            for operand in (
                node_latent,
                fine_edges,
                fine_sender.reshape(fine // GROUP, GROUP),
                fine_receiver.reshape(fine // GROUP, GROUP),
                edge_in,
                edge_out,
                edge_gain.reshape(1, width),
                coarse_edges,
                coarse_receiver.reshape(coarse // GROUP, GROUP),
            )
        ]
    )
    fine_next, coarse_next, node_next = pl.pallas_call(
        last_kernel,
        out_shape=(
            jax.ShapeDtypeStruct((fine, width), jnp.bfloat16),
            jax.ShapeDtypeStruct((coarse, width), jnp.bfloat16),
            jax.ShapeDtypeStruct((nodes, width), jnp.bfloat16),
        ),
        in_specs=[vmem] * 14,
        out_specs=(hbm, hbm, vmem),
        scratch_shapes=[
            pltpu.VMEM((coarse, width), jnp.bfloat16),
            dma((1 + coarse // LAST,)),
        ],
        compiler_params=pltpu.CompilerParams(vmem_limit_bytes=36 * 2**20),
        cost_estimate=pl.CostEstimate(
            flops=5 * 10**9, bytes_accessed=16 * 2**20, transcendentals=coarse * width
        ),
    )(
        fine_made,
        coarse_edges,
        coarse_peer.reshape(coarse // GROUP, GROUP),
        coarse_row.reshape(coarse // GROUP, GROUP),
        coarse_receiver.reshape(coarse // GROUP, GROUP),
        every,
        coarse_base,
        total,
        edge_out,
        edge_gain.reshape(1, width),
        node_latent,
        node_in,
        node_out,
        node_gain.reshape(1, width),
    )
    return (node_next, fine_next, coarse_next)


def with_halo(cells, sides, width, closed):
    for axis, dim in sides:
        count = lax.axis_size(axis)
        ends = count if closed else count - 1
        head = lax.slice_in_dim(cells, 0, width, axis=dim)
        tail = lax.slice_in_dim(cells, cells.shape[dim] - width, cells.shape[dim], axis=dim)
        cells = jnp.concatenate(
            [
                lax.ppermute(tail, axis, [(i, (i + 1) % count) for i in range(ends)]),
                cells,
                lax.ppermute(head, axis, [((i + 1) % count, i) for i in range(ends)]),
            ],
            axis=dim,
        )
    return cells


def layer_norm(values, gain):
    mean = jnp.mean(values, axis=-1, keepdims=True)
    centred = values - mean
    scale = lax.rsqrt(jnp.mean(centred * centred, axis=-1, keepdims=True) + 1e-05)
    return centred * scale * gain


def select_rows(table, picks):
    picker = (picks[:, None] == jnp.arange(table.shape[0], dtype=jnp.int32)[None, :]).astype(
        jnp.bfloat16
    )
    return jnp.dot(picker, table, preferred_element_type=jnp.float32).astype(jnp.bfloat16)


def shards(
    node_latent,
    fine_edges,
    coarse_edges,
    fine_sender,
    fine_receiver,
    coarse_peer,
    coarse_row,
    coarse_receiver,
    edge_in,
    edge_out,
    edge_gain,
    node_in,
    node_out,
    node_gain,
):
    node_count = node_latent.shape[0]
    width = node_latent.shape[1]
    coarse_count = node_count // 4
    fine_count = fine_edges.shape[0]
    lon_size = lax.axis_size("lon")
    lat_size = lax.axis_size("lat")
    lon_here = lax.axis_index("lon")
    lat_here = lax.axis_index("lat")
    grid_lon = node_count // GRID_LAT
    block = node_latent.reshape(grid_lon, GRID_LAT, width)
    sectors = with_halo(block, (("lon", 0),), 1, True)
    square = with_halo(sectors, (("lat", 1),), 1, False)
    beside_all = square.reshape((grid_lon + 2) * (GRID_LAT + 2), width)
    source = fine_sender // node_count
    row_index = fine_sender % node_count
    lon_shift = (source // lat_size - lon_here + 1 + lon_size) % lon_size - 1
    lat_shift = source % lat_size - lat_here
    place_i = row_index // GRID_LAT + 1 + lon_shift * grid_lon
    place_j = row_index % GRID_LAT + 1 + lat_shift * GRID_LAT
    local_sender = place_i * (GRID_LAT + 2) + place_j
    near = select_rows(beside_all, local_sender)
    peers = coarse_peer[:, 0]
    everyone = lax.all_gather(node_latent[:coarse_count], ("lon", "lat"), axis=0, tiled=True)
    far = jnp.take(everyone, peers * coarse_count + coarse_row, axis=0)
    targets = jnp.concatenate([fine_receiver, coarse_receiver], axis=0)
    edges = jnp.concatenate([fine_edges, coarse_edges], axis=0)
    senders = jnp.concatenate([near, far], axis=0)
    receivers = select_rows(node_latent, targets)
    joined = jnp.concatenate([edges, senders, receivers], axis=1)
    edge_hidden = jax.nn.silu(jnp.dot(joined, edge_in, preferred_element_type=jnp.float32)).astype(
        jnp.bfloat16
    )
    edge_change = layer_norm(
        jnp.dot(edge_hidden, edge_out, preferred_element_type=jnp.float32), edge_gain
    )
    message = edge_change.astype(jnp.bfloat16)
    edge_next = (edges.astype(jnp.float32) + edge_change).astype(jnp.bfloat16)
    selector = (jnp.arange(node_count, dtype=jnp.int32)[:, None] == targets[None, :]).astype(
        jnp.bfloat16
    )
    gathered = jnp.dot(selector, message, preferred_element_type=jnp.float32).astype(jnp.bfloat16)
    node_joined = jnp.concatenate([node_latent, gathered], axis=1)
    node_hidden = jax.nn.silu(
        jnp.dot(node_joined, node_in, preferred_element_type=jnp.float32)
    ).astype(jnp.bfloat16)
    node_change = layer_norm(
        jnp.dot(node_hidden, node_out, preferred_element_type=jnp.float32), node_gain
    )
    node_next = (node_latent.astype(jnp.float32) + node_change).astype(jnp.bfloat16)
    return (node_next, edge_next[:fine_count], edge_next[fine_count:])


def solution(mesh):
    small = mesh.shape["lon"] == 4 and mesh.shape["lat"] == 4
    return jax.shard_map(
        fast_shards if small else shards,
        mesh=mesh,
        in_specs=(
            P(("groups", "lon", "lat"), None),
            P(("groups", "lon", "lat"), None),
            P(("groups", "lon", "lat"), None),
            P(("groups", "lon", "lat")),
            P(("groups", "lon", "lat")),
            P(("groups", "lon", "lat"), None),
            P(("groups", "lon", "lat")),
            P(("groups", "lon", "lat")),
            P(),
            P(),
            P(),
            P(),
            P(),
            P(),
        ),
        out_specs=(
            P(("groups", "lon", "lat"), None),
            P(("groups", "lon", "lat"), None),
            P(("groups", "lon", "lat"), None),
        ),
        check_vma=False,
    )
```
